256 devices in a mesh: chan: 128 (over z, x, y_lo, core), pix: 2 (over y_hi).
Axes of the slice: x: 4, y: 4 (y_hi: 2, y_lo: 2; y = y_hi * 2 + y_lo), z: 8, core: 2. Of those that a mesh axis runs over, the one named last changes fastest.
Arguments:
- cube: float32 [4096, 16384], P('pix', 'chan'), as said below
- windows: int32 [8], replicated, may hold values from 1 to 1024, as said below
- mask: int32 [16384], replicated, may hold values from 0 to 1, as said below
Outputs:
- subtracted: float32 [4096, 16384], P('pix', 'chan')
The draws below stay inside these ranges and needn't reach their ends.
Inputs may be any that keep to these rules, and one draw needn't show every extreme that they name: windows[0] is 1024 and windows[7] is 1; for 0 < k < 7, windows[k] is at most 1024 halved k times (rounded down) and more than three quarters of that, but 1 or more. `mask`: zero on 8 disjoint ranges of 256 to 512 channels each, one elsewhere; the k-th range lies inside channels k * 2048 to (k + 1) * 2048 - 1, at least 512 channels from that slot's edges, and at least 1024 channels from either end of the band. `cube`: each spectrum is a smooth continuum of low order plus noise whose level varies from channel to channel.
All inputs are finite; a program needn't handle non-finite values.
Results may differ from the reference program's by a relative error of at most 0.00021.
Values sent between devices are 32-bit elements; how exact they have to be, the bound alone decides.
No kernel may reach another device: no remote copies, remote signals or barrier semaphores. Data moves between devices by JAX's collectives and lax.ppermute only.
A program may use at most 64 MiB of HBM per device.

```python
import jax
import jax.numpy as jnp
from jax import lax

NC = 16384
TERMS = 16
PASSES = 8
WMAX = 1024
PIX_DEV = 16
NPIX = 4096


def draw_cube(key, part):
    keys = jax.random.split(key, 4)
    xvals = (2.0 * jnp.arange(NC).astype(jnp.float32) + 1.0) / NC - 1.0
    table = jnp.stack([jnp.ones_like(xvals), xvals, 1.5 * xvals * xvals - 0.5, 2.5 * xvals ** 3 - 1.5 * xvals], axis=0)
    level = jax.random.uniform(keys[0], (NPIX, 1), jnp.float32, 3.0, 10.0)
    slopes = jax.random.normal(keys[1], (NPIX, 3), jnp.float32)
    coefs = jnp.concatenate([level, slopes], axis=1)
    continuum = coefs @ table
    chan_scale = jnp.exp(jax.random.uniform(keys[2], (1, NC), jnp.float32, jnp.log(0.5), jnp.log(2.0)))
    noise = jax.random.normal(keys[3], (NPIX, NC), jnp.float32)
    return (continuum + noise * chan_scale).astype(jnp.float32)


def draw_windows(key, part):
    steps = jnp.arange(PASSES, dtype=jnp.int32)
    base = jnp.right_shift(jnp.int32(WMAX), steps)
    spread = jnp.maximum(1, jnp.right_shift(jnp.int32(WMAX), steps + 2))
    jitter = jax.random.randint(key, (PASSES,), 0, spread, jnp.int32)
    widths = jnp.maximum(1, base - jitter)
    widths = widths.at[0].set(WMAX)
    widths = widths.at[PASSES - 1].set(1)
    return widths.astype(jnp.int32)


def draw_mask(key, part):
    keys = jax.random.split(key, 2)
    slot = NC // 8
    slots = jnp.arange(8, dtype=jnp.int32)[:, None]
    spans = jax.random.randint(keys[0], (8, 1), NC // 64, NC // 32 + 1, jnp.int32)
    low_margin = jnp.where(slots == 0, NC // 16, NC // 32).astype(jnp.int32)
    high_margin = jnp.where(slots == 7, NC // 16, NC // 32).astype(jnp.int32)
    room = slot - low_margin - high_margin - spans + 1
    offsets = jax.random.randint(keys[1], (8, 1), 0, 1 << 20, jnp.int32) % room
    starts = slots * slot + low_margin + offsets
    column = jnp.arange(NC, dtype=jnp.int32)[None, :]
    inside = (column >= starts) & (column < starts + spans)
    return (1 - jnp.any(inside, axis=0).astype(jnp.int32)).astype(jnp.int32)


def setup_inputs(seed: int = 0) -> dict:
    key_list = jax.random.split(jax.random.key(seed), 4)
    cube = draw_cube(jax.random.fold_in(key_list[3], 71), 0)
    windows = draw_windows(jax.random.fold_in(key_list[3], 71), 0)
    mask = draw_mask(jax.random.fold_in(key_list[3], 71), 0)
    return {"cube": cube, "windows": windows, "mask": mask}


def legendre(xvals):
    rows = [jnp.ones_like(xvals), xvals]
    for order in range(1, TERMS - 1):
        rows.append(((2.0 * order + 1.0) * xvals * rows[order] - order * rows[order - 1]) / (order + 1.0))
    return jnp.stack(rows[:TERMS], axis=0)

def snip(spectra, windows):
    count = spectra.shape[1]
    column = lax.broadcasted_iota(jnp.int32, (1, count), 1)
    for step in range(PASSES):
        width = windows[step]
        padded = jnp.pad(spectra, ((0, 0), (WMAX, WMAX)))
        lower = lax.dynamic_slice_in_dim(padded, (WMAX - width).astype(jnp.int32), count, 1)
        upper = lax.dynamic_slice_in_dim(padded, (WMAX + width).astype(jnp.int32), count, 1)
        inside = (column >= width) & (column < count - width)
        spectra = jnp.where(inside, jnp.minimum(spectra, 0.5 * (lower + upper)), spectra)
    return spectra

def reference(cube, windows, mask):
    xvals = (2.0 * jnp.arange(NC, dtype=jnp.int32).astype(jnp.float32) + 1.0) / NC - 1.0
    table = legendre(xvals)
    weighted = table * mask.astype(jnp.float32)[None, :]
    gram = jnp.dot(weighted, table.T, precision=lax.Precision.HIGHEST)
    factor = jnp.linalg.cholesky(gram)

    def one_block(block):
        baseline = snip(block, windows)
        rhs = jnp.dot(weighted, baseline.T, precision=lax.Precision.HIGHEST)
        middle = lax.linalg.triangular_solve(factor, rhs, left_side=True, lower=True)
        coef = lax.linalg.triangular_solve(factor, middle, left_side=True, lower=True, transpose_a=True)
        return block - jnp.dot(coef.T, table, precision=lax.Precision.HIGHEST)
    blocks = cube.reshape(NPIX // PIX_DEV, PIX_DEV, NC)
    return lax.map(one_block, blocks).reshape(NPIX, NC)
```

```python
import functools

import jax
import jax.numpy as jnp
from jax import lax
from jax.experimental import pallas as pl
from jax.experimental.pallas import tpu as pltpu
from jax.sharding import PartitionSpec as P

TERMS = 16
PASSES = 8
LANES = 128
PAD = 8
CHUNK = 2048
GROUP = 4
HIGHEST = lax.Precision.HIGHEST


def legendre_rows(xvals):
    rows = [jnp.ones_like(xvals), xvals]
    for order in range(1, TERMS - 1):
        rows.append(
            ((2.0 * order + 1.0) * xvals * rows[order] - order * rows[order - 1])
            * (1.0 / (order + 1.0))
        )
    return rows


def inverse(matrix):
    row = lax.broadcasted_iota(jnp.int32, (TERMS, TERMS), 0)
    lane = lax.broadcasted_iota(jnp.int32, (TERMS, TERMS), 1)
    left, right = matrix, (row == lane).astype(jnp.float32)
    for k in range(TERMS):
        column = jnp.sum(jnp.where(lane == k, left, 0.0), axis=1, keepdims=True)
        scale = 1.0 / column[k : k + 1, :]
        left_k, right_k = left[k : k + 1, :] * scale, right[k : k + 1, :] * scale
        left = jnp.where(row == k, left_k, left - column * left_k)
        right = jnp.where(row == k, right_k, right - column * right_k)
    return right


def prepare_kernel(mask_ref, folded_ref, table, weighted):
    total = mask_ref.shape[1]
    gram = jnp.zeros((TERMS, TERMS), jnp.float32)
    for start in range(0, total, CHUNK):
        part = slice(start, start + CHUNK)
        index = lax.broadcasted_iota(jnp.int32, (1, CHUNK), 1) + start
        xvals = (2.0 * index.astype(jnp.float32) + 1.0) / total - 1.0
        keep = mask_ref[:, part].astype(jnp.float32)
        for term, values in enumerate(legendre_rows(xvals)):
            table[term : term + 1, part] = values
            weighted[term : term + 1, part] = values * keep
        gram = gram + lax.dot_general(
            weighted[:, part],
            table[:, part],
            (((1,), (1,)), ((), ())),
            precision=HIGHEST,
            preferred_element_type=jnp.float32,
        )
    inv = inverse(gram)
    for start in range(0, total, CHUNK):
        part = slice(start, start + CHUNK)
        folded_ref[:, part] = jnp.dot(
            inv, weighted[:, part], precision=HIGHEST, preferred_element_type=jnp.float32
        )


def snip_fit_kernel(windows_ref, spectra_ref, folded_ref, coef_ref, first, second):
    n_chan, pix, _ = spectra_ref.shape
    edge = jnp.full((PAD, pix, LANES), jnp.inf, jnp.float32)
    for buffer in (first, second):
        buffer[0:PAD] = edge
        buffer[PAD + n_chan : PAD + n_chan + PAD] = edge

    far = 1024 // LANES
    first[PAD : PAD + far] = spectra_ref[0:far]
    first[PAD + n_chan - far : PAD + n_chan] = spectra_ref[n_chan - far : n_chan]

    @pl.loop(0, (n_chan - 2 * far) // GROUP)
    def _(step):
        base = far + step * GROUP
        for u in range(GROUP):
            c = base + u
            first[PAD + c] = jnp.minimum(
                spectra_ref[c], 0.5 * (spectra_ref[c - far] + spectra_ref[c + far])
            )

    lane = lax.broadcasted_iota(jnp.int32, (pix, LANES), 1)
    source, target = first, second
    for k in range(1, PASSES - 1):
        width = windows_ref[k]
        whole, rest = lax.shift_right_logical(width, 7), width & (LANES - 1)
        up_shift = (LANES - rest) & (LANES - 1)
        up_mask, low_mask = lane >= rest, lane < LANES - rest

        @pl.loop(0, n_chan // GROUP)
        def _(step, source=source, target=target, whole=whole, rest=rest,
              up_shift=up_shift, up_mask=up_mask, low_mask=low_mask):
            base = PAD + step * GROUP
            above = [source[base + whole + u] for u in range(GROUP + 1)]
            below = [source[base - whole + u - 1] for u in range(GROUP + 1)]
            for u in range(GROUP):
                upper = pltpu.roll(jnp.where(up_mask, above[u], above[u + 1]), up_shift, 1)
                lower = pltpu.roll(jnp.where(low_mask, below[u + 1], below[u]), rest, 1)
                target[base + u] = jnp.minimum(source[base + u], 0.5 * (lower + upper))

        source, target = target, source

    up_mask, low_mask = lane >= 1, lane < LANES - 1

    def fit(c, sums):
        left, here, right = source[PAD - 1 + c], source[PAD + c], source[PAD + 1 + c]
        upper = pltpu.roll(jnp.where(up_mask, here, right), LANES - 1, 1)
        lower = pltpu.roll(jnp.where(low_mask, here, left), 1, 1)
        base = jnp.minimum(here, 0.5 * (lower + upper))
        part = pl.ds(pl.multiple_of(c * LANES, LANES), LANES)
        return tuple(
            sums[term] + folded_ref[term : term + 1, part] * base for term in range(TERMS)
        )

    sums = lax.fori_loop(
        0, n_chan, fit, tuple(jnp.zeros((pix, LANES), jnp.float32) for _ in range(TERMS))
    )
    stacked = jnp.concatenate(sums, axis=0)
    coefs = lax.dot_general(
        jnp.ones((8, LANES), jnp.float32),
        stacked,
        (((1,), (1,)), ((), ())),
        precision=HIGHEST,
        preferred_element_type=jnp.float32,
    )
    half = coefs.shape[1] // 2
    pair = jnp.concatenate([coefs[0:1, :half], coefs[0:1, half:]], axis=0)
    coef_ref[...] = jnp.broadcast_to(pair[None], coef_ref.shape)


def subtract_kernel(start_ref, coef_ref, cube_ref, out_ref, left):
    n_chan = coef_ref.shape[0]
    wide = 2 * LANES
    pix = wide // TERMS
    total = n_chan * LANES
    index = lax.broadcasted_iota(jnp.int32, (pix, LANES), 1) + start_ref[0]
    xvals = (2.0 * index.astype(jnp.float32) + 1.0) / total - 1.0
    table = jnp.concatenate(legendre_rows(xvals), axis=0)
    row = lax.broadcasted_iota(jnp.int32, (pix, LANES), 0)
    lane = lax.broadcasted_iota(jnp.int32, (pix, LANES), 1)
    own = (lane & (pix - 1)) == row
    step = 16
    for block in range(0, n_chan, step):
        for u in range(step):
            for h in range(2):
                values = jnp.broadcast_to(coef_ref[block + u, h : h + 1, :], (pix, LANES))
                left[u * pix : (u + 1) * pix, h * LANES : (h + 1) * LANES] = jnp.where(
                    own, values, 0.0
                )
        rows = slice(block * pix, (block + step) * pix)
        out_ref[rows] = cube_ref[rows] - jnp.dot(
            left[...], table, precision=HIGHEST, preferred_element_type=jnp.float32
        )


def params():
    return pltpu.CompilerParams(vmem_limit_bytes=32 * 1024 * 1024)


def per_device(cube, windows, mask):
    ch_dev = cube.shape[1]
    n_chan = lax.axis_size("chan")
    total = ch_dev * n_chan
    pix = cube.shape[0] // n_chan
    vmem = pl.BlockSpec(memory_space=pltpu.VMEM)
    smem = pl.BlockSpec(memory_space=pltpu.SMEM)

    spectra = lax.all_to_all(
        cube.reshape(n_chan, pix, ch_dev), "chan", split_axis=0, concat_axis=0, tiled=True
    )
    folded = pl.pallas_call(
        prepare_kernel,
        out_shape=jax.ShapeDtypeStruct((TERMS, total), jnp.float32),
        in_specs=[vmem],
        out_specs=vmem,
        scratch_shapes=[pltpu.VMEM((TERMS, total), jnp.float32)] * 2,
        compiler_params=params(),
        cost_estimate=pl.CostEstimate(
            flops=20_000_000, bytes_accessed=total * 68, transcendentals=0
        ),
    )(mask.reshape(1, total))
    coefs = pl.pallas_call(
        snip_fit_kernel,
        out_shape=jax.ShapeDtypeStruct((n_chan, 2, LANES), jnp.float32),
        in_specs=[smem, vmem, vmem],
        out_specs=vmem,
        scratch_shapes=[pltpu.VMEM((n_chan + 2 * PAD, pix, LANES), jnp.float32)] * 2,
        compiler_params=params(),
    )(windows, spectra, folded)
    gathered = lax.all_to_all(coefs, "chan", split_axis=0, concat_axis=0, tiled=True)
    start = (lax.axis_index("chan") * ch_dev).astype(jnp.int32).reshape(1)
    return pl.pallas_call(
        subtract_kernel,
        out_shape=jax.ShapeDtypeStruct(cube.shape, jnp.float32),
        in_specs=[smem, vmem, vmem],
        out_specs=vmem,
        scratch_shapes=[pltpu.VMEM((16 * pix, 2 * LANES), jnp.float32)],
        compiler_params=params(),
    )(start, gathered, cube)


def solution(mesh):
    placed = (P("pix", "chan"), P(), P())
    return jax.shard_map(
        per_device, mesh=mesh, in_specs=placed, out_specs=P("pix", "chan"), check_vma=False
    )
```

```python
import functools

import jax
import jax.numpy as jnp
from jax import lax
from jax.experimental import pallas as pl
from jax.experimental.pallas import tpu as pltpu
from jax.sharding import PartitionSpec as P

TERMS = 16
PASSES = 8
LANES = 128
WMAX = 1024
HALO = WMAX // 2
SEGMENTS = 8
CHUNK = 2048
HIGHEST = lax.Precision.HIGHEST


def legendre_rows(xvals):
    rows = [jnp.ones_like(xvals), xvals]
    for order in range(1, TERMS - 1):
        rows.append(
            ((2.0 * order + 1.0) * xvals * rows[order] - order * rows[order - 1])
            * (1.0 / (order + 1.0))
        )
    return rows


def inverse(matrix):
    row = lax.broadcasted_iota(jnp.int32, (TERMS, TERMS), 0)
    lane = lax.broadcasted_iota(jnp.int32, (TERMS, TERMS), 1)
    left, right = matrix, (row == lane).astype(jnp.float32)
    for k in range(TERMS):
        column = jnp.sum(jnp.where(lane == k, left, 0.0), axis=1, keepdims=True)
        scale = 1.0 / column[k : k + 1, :]
        left_k, right_k = left[k : k + 1, :] * scale, right[k : k + 1, :] * scale
        left = jnp.where(row == k, left_k, left - column * left_k)
        right = jnp.where(row == k, right_k, right - column * right_k)
    return right


def split(values):
    high = values.astype(jnp.bfloat16)
    return high, (values - high.astype(jnp.float32)).astype(jnp.bfloat16)


def dot(left, right):
    return jnp.dot(left, right, preferred_element_type=jnp.float32)


def prepare_kernel(mask_ref, high_ref, low_ref, table, weighted):
    total = mask_ref.shape[1]
    gram = jnp.zeros((TERMS, TERMS), jnp.float32)
    for start in range(0, total, CHUNK):
        part = slice(start, start + CHUNK)
        index = lax.broadcasted_iota(jnp.int32, (1, CHUNK), 1) + start
        xvals = (2.0 * index.astype(jnp.float32) + 1.0) / total - 1.0
        keep = mask_ref[:, part].astype(jnp.float32)
        for term, values in enumerate(legendre_rows(xvals)):
            table[term : term + 1, part] = values
            weighted[term : term + 1, part] = values * keep
        gram = gram + lax.dot_general(
            weighted[:, part],
            table[:, part],
            (((1,), (1,)), ((), ())),
            precision=HIGHEST,
            preferred_element_type=jnp.float32,
        )
    inv = inverse(gram)
    count = total // SEGMENTS
    for segment in range(SEGMENTS):
        folded = jnp.dot(
            inv,
            weighted[:, segment * count : (segment + 1) * count],
            precision=HIGHEST,
            preferred_element_type=jnp.float32,
        )
        rows = slice(segment * TERMS, (segment + 1) * TERMS)
        high_ref[rows], low_ref[rows] = split(folded)


def snip_fit_kernel(windows_ref, spectra_ref, high_ref, low_ref, coef_ref, first, second, hi, lo):
    n_chan, pix, _ = spectra_ref.shape
    blocks = n_chan // SEGMENTS
    rows = blocks * LANES
    half = blocks // 2
    lane = lax.broadcasted_iota(jnp.int32, (LANES, LANES), 1)

    def from_below(values):
        return jnp.where(
            lane[: values.shape[0]] < pix, jnp.inf, pltpu.roll(values, pix, 1)
        )

    def from_above(values):
        return jnp.where(
            lane[: values.shape[0]] >= LANES - pix, jnp.inf, pltpu.roll(values, LANES - pix, 1)
        )

    def turned(block):
        return jnp.concatenate(
            [spectra_ref[segment * blocks + block] for segment in range(SEGMENTS)], axis=0
        ).T

    for block in range(half):
        low, high = turned(block), turned(block + half)
        first[pl.ds(HALO + block * LANES, LANES)] = jnp.minimum(
            low, 0.5 * (from_below(high) + high)
        )
        first[pl.ds(HALO + (block + half) * LANES, LANES)] = jnp.minimum(
            high, 0.5 * (low + from_above(low))
        )

    source, target = first, second
    for k in range(1, PASSES):
        reach = max(8, WMAX >> k)
        for start in range(0, reach, LANES):
            count = min(LANES, reach)
            source[HALO - reach + start : HALO - reach + start + count] = from_below(
                source[HALO + rows - reach + start : HALO + rows - reach + start + count]
            )
            source[HALO + rows + start : HALO + rows + start + count] = from_above(
                source[HALO + start : HALO + start + count]
            )
        width = windows_ref[k] if k < PASSES - 1 else 1
        for start in range(0, rows, CHUNK):
            lower = source[pl.ds(HALO + start - width, CHUNK)]
            upper = source[pl.ds(HALO + start + width, CHUNK)]
            here = source[HALO + start : HALO + start + CHUNK]
            values = jnp.minimum(here, 0.5 * (lower + upper))
            if k < PASSES - 1:
                target[HALO + start : HALO + start + CHUNK] = values
            else:
                hi[start : start + CHUNK], lo[start : start + CHUNK] = split(values)
        source, target = target, source

    products = dot(high_ref[...], hi[...]) + (
        dot(low_ref[...], hi[...]) + dot(high_ref[...], lo[...])
    )
    lane = lax.broadcasted_iota(jnp.int32, (TERMS, LANES), 1)
    term = lax.broadcasted_iota(jnp.int32, (TERMS, LANES), 0)
    coefs = jnp.zeros((TERMS, LANES), jnp.float32)
    for segment in range(SEGMENTS):
        coefs = coefs + jnp.where(
            (lane // pix) == segment, products[segment * TERMS : (segment + 1) * TERMS], 0.0
        )
    shift = LANES // 2
    while shift >= pix:
        coefs = coefs + pltpu.roll(coefs, shift, 1)
        shift //= 2
    coefs = jnp.where((lane // pix) == (term % 8), coefs, 0.0)
    pair = jnp.concatenate(
        [jnp.sum(coefs[:8], axis=0, keepdims=True), jnp.sum(coefs[8:], axis=0, keepdims=True)],
        axis=0,
    )
    coef_ref[...] = jnp.broadcast_to(pair[None], coef_ref.shape)


def subtract_kernel(start_ref, coef_ref, cube_ref, out_ref, left):
    n_chan = coef_ref.shape[0]
    wide = 2 * LANES
    pix = wide // TERMS
    total = n_chan * LANES
    index = lax.broadcasted_iota(jnp.int32, (pix, LANES), 1) + start_ref[0]
    xvals = (2.0 * index.astype(jnp.float32) + 1.0) / total - 1.0
    table = jnp.concatenate(legendre_rows(xvals), axis=0)
    row = lax.broadcasted_iota(jnp.int32, (pix, LANES), 0)
    lane = lax.broadcasted_iota(jnp.int32, (pix, LANES), 1)
    own = (lane & (pix - 1)) == row
    step = 16
    for block in range(0, n_chan, step):
        for u in range(step):
            for h in range(2):
                values = jnp.broadcast_to(coef_ref[block + u, h : h + 1, :], (pix, LANES))
                left[u * pix : (u + 1) * pix, h * LANES : (h + 1) * LANES] = jnp.where(
                    own, values, 0.0
                )
        rows = slice(block * pix, (block + step) * pix)
        out_ref[rows] = cube_ref[rows] - jnp.dot(
            left[...], table, precision=HIGHEST, preferred_element_type=jnp.float32
        )


def params():
    return pltpu.CompilerParams(vmem_limit_bytes=32 * 1024 * 1024)


def per_device(cube, windows, mask):
    ch_dev = cube.shape[1]
    n_chan = lax.axis_size("chan")
    total = ch_dev * n_chan
    pix = cube.shape[0] // n_chan
    vmem = pl.BlockSpec(memory_space=pltpu.VMEM)
    smem = pl.BlockSpec(memory_space=pltpu.SMEM)

    spectra = lax.all_to_all(
        cube.reshape(n_chan, pix, ch_dev), "chan", split_axis=0, concat_axis=0, tiled=True
    )
    rows = total // SEGMENTS
    high, low = pl.pallas_call(
        prepare_kernel,
        out_shape=[jax.ShapeDtypeStruct((SEGMENTS * TERMS, rows), jnp.bfloat16)] * 2,
        in_specs=[vmem],
        out_specs=[vmem, vmem],
        scratch_shapes=[pltpu.VMEM((TERMS, total), jnp.float32)] * 2,
        compiler_params=params(),
        cost_estimate=pl.CostEstimate(
            flops=20_000_000, bytes_accessed=total * 68, transcendentals=0
        ),
    )(mask.reshape(1, total))
    coefs = pl.pallas_call(
        snip_fit_kernel,
        out_shape=jax.ShapeDtypeStruct((n_chan, 2, LANES), jnp.float32),
        in_specs=[smem, vmem, vmem, vmem],
        out_specs=vmem,
        scratch_shapes=[pltpu.VMEM((rows + 2 * HALO, LANES), jnp.float32)] * 2
        + [pltpu.VMEM((rows, LANES), jnp.bfloat16)] * 2,
        compiler_params=params(),
    )(windows, spectra, high, low)
    gathered = lax.all_to_all(coefs, "chan", split_axis=0, concat_axis=0, tiled=True)
    start = (lax.axis_index("chan") * ch_dev).astype(jnp.int32).reshape(1)
    return pl.pallas_call(
        subtract_kernel,
        out_shape=jax.ShapeDtypeStruct(cube.shape, jnp.float32),
        in_specs=[smem, vmem, vmem],
        out_specs=vmem,
        scratch_shapes=[pltpu.VMEM((16 * pix, 2 * LANES), jnp.float32)],
        compiler_params=params(),
    )(start, gathered, cube)


def solution(mesh):
    placed = (P("pix", "chan"), P(), P())
    return jax.shard_map(
        per_device, mesh=mesh, in_specs=placed, out_specs=P("pix", "chan"), check_vma=False
    )
```

```python
import functools

import jax
import jax.numpy as jnp
from jax import lax
from jax.experimental import pallas as pl
from jax.experimental.pallas import tpu as pltpu
from jax.sharding import PartitionSpec as P

TERMS = 16
PASSES = 8
LANES = 128
WMAX = 1024
HALO = WMAX // 2
SEGMENTS = 8
CHUNK = 2048
WRITES = 8
HIGHEST = lax.Precision.HIGHEST


def legendre_rows(xvals):
    rows = [jnp.ones_like(xvals), xvals]
    for order in range(1, TERMS - 1):
        rows.append(
            ((2.0 * order + 1.0) * xvals * rows[order] - order * rows[order - 1])
            * (1.0 / (order + 1.0))
        )
    return rows


def inverse(matrix):
    row = lax.broadcasted_iota(jnp.int32, (TERMS, TERMS), 0)
    lane = lax.broadcasted_iota(jnp.int32, (TERMS, TERMS), 1)
    left, right = matrix, (row == lane).astype(jnp.float32)
    for k in range(TERMS):
        column = jnp.sum(jnp.where(lane == k, left, 0.0), axis=1, keepdims=True)
        scale = 1.0 / column[k : k + 1, :]
        left_k, right_k = left[k : k + 1, :] * scale, right[k : k + 1, :] * scale
        left = jnp.where(row == k, left_k, left - column * left_k)
        right = jnp.where(row == k, right_k, right - column * right_k)
    return right


def split(values):
    high = values.astype(jnp.bfloat16)
    return high, (values - high.astype(jnp.float32)).astype(jnp.bfloat16)


def dot(left, right):
    return jnp.dot(left, right, preferred_element_type=jnp.float32)


def prepare_kernel(start_ref, windows_ref, mask_ref, high_ref, low_ref, local_ref, widths_ref,
                   table, weighted):
    total = mask_ref.shape[1]
    row = lax.broadcasted_iota(jnp.int32, widths_ref.shape, 0)
    widths = jnp.zeros(widths_ref.shape, jnp.int32)
    for k in range(PASSES):
        widths = jnp.where(row == k, windows_ref[k], widths)
    widths_ref[...] = widths

    pix = local_ref.shape[0] // (2 * TERMS)
    index = lax.broadcasted_iota(jnp.int32, (pix, LANES), 1) + start_ref[0]
    xvals = (2.0 * index.astype(jnp.float32) + 1.0) / total - 1.0
    for term, values in enumerate(legendre_rows(xvals)):
        high, low = split(values)
        for half in range(2):
            rows = slice((half * TERMS + term) * pix, (half * TERMS + term + 1) * pix)
            local_ref[rows, :LANES], local_ref[rows, LANES:] = high, low

    gram = jnp.zeros((TERMS, TERMS), jnp.float32)
    for start in range(0, total, CHUNK):
        part = slice(start, start + CHUNK)
        index = lax.broadcasted_iota(jnp.int32, (1, CHUNK), 1) + start
        xvals = (2.0 * index.astype(jnp.float32) + 1.0) / total - 1.0
        keep = mask_ref[:, part].astype(jnp.float32)
        for term, values in enumerate(legendre_rows(xvals)):
            table[term : term + 1, part] = values
            weighted[term : term + 1, part] = values * keep
        gram = gram + lax.dot_general(
            weighted[:, part],
            table[:, part],
            (((1,), (1,)), ((), ())),
            precision=HIGHEST,
            preferred_element_type=jnp.float32,
        )
    inv = inverse(gram)
    count = total // SEGMENTS
    for segment in range(SEGMENTS):
        folded = jnp.dot(
            inv,
            weighted[:, segment * count : (segment + 1) * count],
            precision=HIGHEST,
            preferred_element_type=jnp.float32,
        )
        rows = slice(segment * TERMS, (segment + 1) * TERMS)
        high_ref[rows], low_ref[rows] = split(folded)


def snip_fit_kernel(widths_ref, spectra_ref, high_ref, low_ref, coef_ref,
                    first, second, hi, lo, widths, arrived):
    fetch = pltpu.make_async_copy(widths_ref, widths, arrived)
    fetch.start()
    n_chan, pix, _ = spectra_ref.shape
    blocks = n_chan // SEGMENTS
    rows = blocks * LANES
    half = blocks // 2
    lane = lax.broadcasted_iota(jnp.int32, (LANES, LANES), 1)

    def from_below(values):
        return jnp.where(
            lane[: values.shape[0]] < pix, jnp.inf, pltpu.roll(values, pix, 1)
        )

    def from_above(values):
        return jnp.where(
            lane[: values.shape[0]] >= LANES - pix, jnp.inf, pltpu.roll(values, LANES - pix, 1)
        )

    def turned(block):
        return jnp.concatenate(
            [spectra_ref[segment * blocks + block] for segment in range(SEGMENTS)], axis=0
        ).T

    for block in range(half):
        low, high = turned(block), turned(block + half)
        first[pl.ds(HALO + block * LANES, LANES)] = jnp.minimum(
            low, 0.5 * (from_below(high) + high)
        )
        first[pl.ds(HALO + (block + half) * LANES, LANES)] = jnp.minimum(
            high, 0.5 * (low + from_above(low))
        )

    fetch.wait()
    source, target = first, second
    for k in range(1, PASSES):
        reach = max(8, WMAX >> k)
        for start in range(0, reach, LANES):
            count = min(LANES, reach)
            source[HALO - reach + start : HALO - reach + start + count] = from_below(
                source[HALO + rows - reach + start : HALO + rows - reach + start + count]
            )
            source[HALO + rows + start : HALO + rows + start + count] = from_above(
                source[HALO + start : HALO + start + count]
            )
        width = widths[k, 0] if k < PASSES - 1 else 1
        for start in range(0, rows, CHUNK):
            lower = source[pl.ds(HALO + start - width, CHUNK)]
            upper = source[pl.ds(HALO + start + width, CHUNK)]
            here = source[HALO + start : HALO + start + CHUNK]
            values = jnp.minimum(here, 0.5 * (lower + upper))
            if k < PASSES - 1:
                target[HALO + start : HALO + start + CHUNK] = values
            else:
                hi[start : start + CHUNK], lo[start : start + CHUNK] = split(values)
        source, target = target, source

    products = dot(high_ref[...], hi[...]) + (
        dot(low_ref[...], hi[...]) + dot(high_ref[...], lo[...])
    )
    lane = lax.broadcasted_iota(jnp.int32, (TERMS, LANES), 1)
    term = lax.broadcasted_iota(jnp.int32, (TERMS, LANES), 0)
    coefs = jnp.zeros((TERMS, LANES), jnp.float32)
    for segment in range(SEGMENTS):
        coefs = coefs + jnp.where(
            (lane // pix) == segment, products[segment * TERMS : (segment + 1) * TERMS], 0.0
        )
    shift = LANES // 2
    while shift >= pix:
        coefs = coefs + pltpu.roll(coefs, shift, 1)
        shift //= 2
    coefs = jnp.where((lane // pix) == (term % 8), coefs, 0.0)
    coef_ref[0:1] = jnp.sum(coefs[:8], axis=0, keepdims=True)
    coef_ref[1:2] = jnp.sum(coefs[8:], axis=0, keepdims=True)


def subtract_kernel(coef_ref, local_ref, cube_ref, out_ref, left, result, sent):
    chips = coef_ref.shape[0]
    pix = local_ref.shape[0] // (2 * TERMS)
    row = lax.broadcasted_iota(jnp.int32, (pix, LANES), 0)
    lane = lax.broadcasted_iota(jnp.int32, (pix, LANES), 1)
    own = (lane & (pix - 1)) == row
    step = 2 * chips // WRITES
    copies = []
    for block in range(WRITES):
        slot = left.at[block % 2]
        for u in range(step):
            chip, core = divmod(block * step + u, 2)
            for half in range(2):
                at = 2 * core + half
                values = jnp.broadcast_to(coef_ref[chip, at : at + 1, :], (pix, LANES))
                high, low = split(jnp.where(own, values, 0.0))
                rows = slice(u * pix, (u + 1) * pix)
                slot[rows, half * LANES : (half + 1) * LANES] = high
                slot[rows, (2 + half) * LANES : (3 + half) * LANES] = low
        fitted = dot(slot[...], local_ref[...])
        rows = pl.ds(block * step * pix, step * pix)
        result[rows] = cube_ref[rows] - (fitted[:, :LANES] + fitted[:, LANES:])
        copy = pltpu.make_async_copy(result.at[rows], out_ref.at[rows], sent.at[block])
        copy.start()
        copies.append(copy)
    for copy in copies:
        copy.wait()


def params():
    return pltpu.CompilerParams(vmem_limit_bytes=32 * 1024 * 1024)


def per_device(cube, windows, mask):
    ch_dev = cube.shape[1]
    n_chan = lax.axis_size("chan")
    total = ch_dev * n_chan
    pix = cube.shape[0] // n_chan
    vmem = pl.BlockSpec(memory_space=pltpu.VMEM)
    smem = pl.BlockSpec(memory_space=pltpu.SMEM)

    spectra = lax.all_to_all(
        cube.reshape(n_chan, pix, ch_dev), "chan", split_axis=0, concat_axis=0, tiled=True
    )
    rows = total // SEGMENTS
    me = lax.axis_index("chan")
    start = (me * ch_dev).astype(jnp.int32).reshape(1)
    high, low, local, widths = pl.pallas_call(
        prepare_kernel,
        out_shape=[jax.ShapeDtypeStruct((SEGMENTS * TERMS, rows), jnp.bfloat16)] * 2
        + [
            jax.ShapeDtypeStruct((2 * TERMS * pix, 2 * LANES), jnp.bfloat16),
            jax.ShapeDtypeStruct((PASSES, LANES), jnp.int32),
        ],
        in_specs=[smem, smem, vmem],
        out_specs=[vmem] * 4,
        scratch_shapes=[pltpu.VMEM((TERMS, total), jnp.float32)] * 2,
        compiler_params=params(),
        cost_estimate=pl.CostEstimate(
            flops=20_000_000, bytes_accessed=total * 68, transcendentals=0
        ),
    )(start, windows, mask.reshape(1, total))
    coefs = pl.pallas_call(
        snip_fit_kernel,
        out_shape=jax.ShapeDtypeStruct((2, LANES), jnp.float32),
        in_specs=[pl.BlockSpec(memory_space=pl.ANY), vmem, vmem, vmem],
        out_specs=vmem,
        scratch_shapes=[pltpu.VMEM((rows + 2 * HALO, LANES), jnp.float32)] * 2
        + [pltpu.VMEM((rows, LANES), jnp.bfloat16)] * 2
        + [pltpu.SMEM((PASSES, LANES), jnp.int32), pltpu.SemaphoreType.DMA],
        compiler_params=params(),
    )(widths, spectra, high, low)

    other = lax.ppermute(coefs, "chan", [(i, i ^ 1) for i in range(n_chan)])
    pair = jnp.where(
        me % 2 == 0, jnp.concatenate([coefs, other]), jnp.concatenate([other, coefs])
    )
    chips = n_chan // 2
    gathered = lax.all_to_all(
        jnp.broadcast_to(pair[None], (chips,) + pair.shape),
        "chan",
        split_axis=0,
        concat_axis=0,
        tiled=True,
        axis_index_groups=[list(range(core, n_chan, 2)) for core in range(2)],
    )
    return pl.pallas_call(
        subtract_kernel,
        out_shape=jax.ShapeDtypeStruct(cube.shape, jnp.float32),
        in_specs=[vmem] * 3,
        out_specs=pl.BlockSpec(memory_space=pl.ANY),
        scratch_shapes=[
            pltpu.VMEM((2, cube.shape[0] // WRITES, 4 * LANES), jnp.bfloat16),
            pltpu.VMEM(cube.shape, jnp.float32),
            pltpu.SemaphoreType.DMA((WRITES,)),
        ],
        compiler_params=params(),
    )(gathered, local, cube)


def solution(mesh):
    placed = (P("pix", "chan"), P(), P())
    return jax.shard_map(
        per_device, mesh=mesh, in_specs=placed, out_specs=P("pix", "chan"), check_vma=False
    )
```

```python
import functools

import jax
import jax.numpy as jnp
from jax import lax
from jax.experimental import pallas as pl
from jax.experimental.pallas import tpu as pltpu
from jax.sharding import PartitionSpec as P

TERMS = 16
PASSES = 8
LANES = 128
WMAX = 1024
HALO = WMAX // 2
SEGMENTS = 8
CHUNK = 2048
WRITES = 8
HIGHEST = lax.Precision.HIGHEST


def exchange_order(n_chan):
    lead = n_chan * 75 // 128
    rest = [(17 * step) % n_chan for step in range(n_chan)]
    return [lead] + [device for device in rest if device != lead]


def chip_order(order):
    return list(dict.fromkeys(device // 2 for device in order))


def legendre_rows(xvals):
    rows = [jnp.ones_like(xvals), xvals]
    for order in range(1, TERMS - 1):
        rows.append(
            ((2.0 * order + 1.0) * xvals * rows[order] - order * rows[order - 1])
            * (1.0 / (order + 1.0))
        )
    return rows


def inverse(matrix):
    row = lax.broadcasted_iota(jnp.int32, (TERMS, TERMS), 0)
    lane = lax.broadcasted_iota(jnp.int32, (TERMS, TERMS), 1)
    left, right = matrix, (row == lane).astype(jnp.float32)
    for k in range(TERMS):
        column = jnp.sum(jnp.where(lane == k, left, 0.0), axis=1, keepdims=True)
        scale = 1.0 / column[k : k + 1, :]
        left_k, right_k = left[k : k + 1, :] * scale, right[k : k + 1, :] * scale
        left = jnp.where(row == k, left_k, left - column * left_k)
        right = jnp.where(row == k, right_k, right - column * right_k)
    return right


def split(values):
    high = values.astype(jnp.bfloat16)
    return high, (values - high.astype(jnp.float32)).astype(jnp.bfloat16)


def dot(left, right):
    return jnp.dot(left, right, preferred_element_type=jnp.float32)


def prepare_kernel(start_ref, windows_ref, mask_ref, high_ref, low_ref, local_ref, widths_ref,
                   table, weighted):
    total = mask_ref.shape[1]
    row = lax.broadcasted_iota(jnp.int32, widths_ref.shape, 0)
    widths = jnp.zeros(widths_ref.shape, jnp.int32)
    for k in range(PASSES):
        widths = jnp.where(row == k, windows_ref[k], widths)
    widths_ref[...] = widths

    pix = local_ref.shape[0] // (2 * TERMS)
    index = lax.broadcasted_iota(jnp.int32, (pix, LANES), 1) + start_ref[0]
    xvals = (2.0 * index.astype(jnp.float32) + 1.0) / total - 1.0
    for term, values in enumerate(legendre_rows(xvals)):
        high, low = split(values)
        for half in range(2):
            rows = slice((half * TERMS + term) * pix, (half * TERMS + term + 1) * pix)
            local_ref[rows, :LANES], local_ref[rows, LANES:] = high, low

    gram = jnp.zeros((TERMS, TERMS), jnp.float32)
    for start in range(0, total, CHUNK):
        part = slice(start, start + CHUNK)
        index = lax.broadcasted_iota(jnp.int32, (1, CHUNK), 1) + start
        xvals = (2.0 * index.astype(jnp.float32) + 1.0) / total - 1.0
        keep = mask_ref[:, part].astype(jnp.float32)
        for term, values in enumerate(legendre_rows(xvals)):
            table[term : term + 1, part] = values
            weighted[term : term + 1, part] = values * keep
        gram = gram + lax.dot_general(
            weighted[:, part],
            table[:, part],
            (((1,), (1,)), ((), ())),
            precision=HIGHEST,
            preferred_element_type=jnp.float32,
        )
    inv = inverse(gram)
    count = total // SEGMENTS
    for segment in range(SEGMENTS):
        folded = jnp.dot(
            inv,
            weighted[:, segment * count : (segment + 1) * count],
            precision=HIGHEST,
            preferred_element_type=jnp.float32,
        )
        rows = slice(segment * TERMS, (segment + 1) * TERMS)
        high_ref[rows], low_ref[rows] = split(folded)


def snip_fit_kernel(widths_ref, spectra_ref, high_ref, low_ref, coef_ref,
                    first, second, hi, lo, widths, arrived):
    fetch = pltpu.make_async_copy(widths_ref, widths, arrived)
    fetch.start()
    n_chan, pix, _ = spectra_ref.shape
    blocks = n_chan // SEGMENTS
    rows = blocks * LANES
    half = blocks // 2
    order = exchange_order(n_chan)
    place = [order.index(device) for device in range(n_chan)]
    lane = lax.broadcasted_iota(jnp.int32, (LANES, LANES), 1)

    def from_below(values):
        return jnp.where(
            lane[: values.shape[0]] < pix, jnp.inf, pltpu.roll(values, pix, 1)
        )

    def from_above(values):
        return jnp.where(
            lane[: values.shape[0]] >= LANES - pix, jnp.inf, pltpu.roll(values, LANES - pix, 1)
        )

    def turned(block):
        return jnp.concatenate(
            [spectra_ref[place[segment * blocks + block]] for segment in range(SEGMENTS)], axis=0
        ).T

    for block in range(half):
        low, high = turned(block), turned(block + half)
        first[pl.ds(HALO + block * LANES, LANES)] = jnp.minimum(
            low, 0.5 * (from_below(high) + high)
        )
        first[pl.ds(HALO + (block + half) * LANES, LANES)] = jnp.minimum(
            high, 0.5 * (low + from_above(low))
        )

    fetch.wait()
    source, target = first, second
    for k in range(1, PASSES):
        reach = max(8, WMAX >> k)
        for start in range(0, reach, LANES):
            count = min(LANES, reach)
            source[HALO - reach + start : HALO - reach + start + count] = from_below(
                source[HALO + rows - reach + start : HALO + rows - reach + start + count]
            )
            source[HALO + rows + start : HALO + rows + start + count] = from_above(
                source[HALO + start : HALO + start + count]
            )
        width = widths[k, 0] if k < PASSES - 1 else 1
        for start in range(0, rows, CHUNK):
            lower = source[pl.ds(HALO + start - width, CHUNK)]
            upper = source[pl.ds(HALO + start + width, CHUNK)]
            here = source[HALO + start : HALO + start + CHUNK]
            values = jnp.minimum(here, 0.5 * (lower + upper))
            if k < PASSES - 1:
                target[HALO + start : HALO + start + CHUNK] = values
            else:
                hi[start : start + CHUNK], lo[start : start + CHUNK] = split(values)
        source, target = target, source

    products = dot(high_ref[...], hi[...]) + (
        dot(low_ref[...], hi[...]) + dot(high_ref[...], lo[...])
    )
    lane = lax.broadcasted_iota(jnp.int32, (TERMS, LANES), 1)
    term = lax.broadcasted_iota(jnp.int32, (TERMS, LANES), 0)
    coefs = jnp.zeros((TERMS, LANES), jnp.float32)
    for segment in range(SEGMENTS):
        coefs = coefs + jnp.where(
            (lane // pix) == segment, products[segment * TERMS : (segment + 1) * TERMS], 0.0
        )
    shift = LANES // 2
    while shift >= pix:
        coefs = coefs + pltpu.roll(coefs, shift, 1)
        shift //= 2
    coefs = jnp.where((lane // pix) == (term % 8), coefs, 0.0)
    coef_ref[0:1] = jnp.sum(coefs[:8], axis=0, keepdims=True)
    coef_ref[1:2] = jnp.sum(coefs[8:], axis=0, keepdims=True)


def subtract_kernel(coef_ref, local_ref, cube_ref, out_ref, left, result, sent):
    chips = coef_ref.shape[0]
    pix = local_ref.shape[0] // (2 * TERMS)
    row = lax.broadcasted_iota(jnp.int32, (pix, LANES), 0)
    lane = lax.broadcasted_iota(jnp.int32, (pix, LANES), 1)
    own = (lane & (pix - 1)) == row
    step = 2 * chips // WRITES
    order = exchange_order(2 * chips)
    leads = chip_order(order)
    copies = []
    for block in range(WRITES):
        slot = left.at[block % 2]
        for u in range(step):
            chip, core = divmod(order[block * step + u], 2)
            chip = leads.index(chip)
            for half in range(2):
                at = 2 * core + half
                values = jnp.broadcast_to(coef_ref[chip, at : at + 1, :], (pix, LANES))
                high, low = split(jnp.where(own, values, 0.0))
                rows = slice(u * pix, (u + 1) * pix)
                slot[rows, half * LANES : (half + 1) * LANES] = high
                slot[rows, (2 + half) * LANES : (3 + half) * LANES] = low
        fitted = dot(slot[...], local_ref[...])
        rows = pl.ds(block * step * pix, step * pix)
        result[rows] = cube_ref[rows] - (fitted[:, :LANES] + fitted[:, LANES:])
        copy = pltpu.make_async_copy(result.at[rows], out_ref.at[rows], sent.at[block])
        copy.start()
        copies.append(copy)
    for copy in copies:
        copy.wait()


def params():
    return pltpu.CompilerParams(vmem_limit_bytes=32 * 1024 * 1024)


def per_device(cube, windows, mask):
    ch_dev = cube.shape[1]
    n_chan = lax.axis_size("chan")
    total = ch_dev * n_chan
    pix = cube.shape[0] // n_chan
    vmem = pl.BlockSpec(memory_space=pltpu.VMEM)
    smem = pl.BlockSpec(memory_space=pltpu.SMEM)

    order = exchange_order(n_chan)
    spectra = lax.all_to_all(
        cube.reshape(n_chan, pix, ch_dev),
        "chan",
        split_axis=0,
        concat_axis=0,
        tiled=True,
        axis_index_groups=[order],
    )
    rows = total // SEGMENTS
    me = lax.axis_index("chan")
    start = (me * ch_dev).astype(jnp.int32).reshape(1)
    high, low, local, widths = pl.pallas_call(
        prepare_kernel,
        out_shape=[jax.ShapeDtypeStruct((SEGMENTS * TERMS, rows), jnp.bfloat16)] * 2
        + [
            jax.ShapeDtypeStruct((2 * TERMS * pix, 2 * LANES), jnp.bfloat16),
            jax.ShapeDtypeStruct((PASSES, LANES), jnp.int32),
        ],
        in_specs=[smem, smem, vmem],
        out_specs=[vmem] * 4,
        scratch_shapes=[pltpu.VMEM((TERMS, total), jnp.float32)] * 2,
        compiler_params=params(),
        cost_estimate=pl.CostEstimate(
            flops=20_000_000, bytes_accessed=total * 68, transcendentals=0
        ),
    )(start, windows, mask.reshape(1, total))
    coefs = pl.pallas_call(
        snip_fit_kernel,
        out_shape=jax.ShapeDtypeStruct((2, LANES), jnp.float32),
        in_specs=[pl.BlockSpec(memory_space=pl.ANY), vmem, vmem, vmem],
        out_specs=vmem,
        scratch_shapes=[pltpu.VMEM((rows + 2 * HALO, LANES), jnp.float32)] * 2
        + [pltpu.VMEM((rows, LANES), jnp.bfloat16)] * 2
        + [pltpu.SMEM((PASSES, LANES), jnp.int32), pltpu.SemaphoreType.DMA],
        compiler_params=params(),
    )(widths, spectra, high, low)

    other = lax.ppermute(coefs, "chan", [(i, i ^ 1) for i in range(n_chan)])
    pair = jnp.where(
        me % 2 == 0, jnp.concatenate([coefs, other]), jnp.concatenate([other, coefs])
    )
    chips = n_chan // 2
    gathered = lax.all_to_all(
        jnp.broadcast_to(pair[None], (chips,) + pair.shape),
        "chan",
        split_axis=0,
        concat_axis=0,
        tiled=True,
        axis_index_groups=[[2 * chip + core for chip in chip_order(order)] for core in range(2)],
    )
    return pl.pallas_call(
        subtract_kernel,
        out_shape=jax.ShapeDtypeStruct(cube.shape, jnp.float32),
        in_specs=[vmem] * 3,
        out_specs=pl.BlockSpec(memory_space=pl.ANY),
        scratch_shapes=[
            pltpu.VMEM((2, cube.shape[0] // WRITES, 4 * LANES), jnp.bfloat16),
            pltpu.VMEM(cube.shape, jnp.float32),
            pltpu.SemaphoreType.DMA((WRITES,)),
        ],
        compiler_params=params(),
    )(gathered, local, cube)


def solution(mesh):
    placed = (P("pix", "chan"), P(), P())
    return jax.shard_map(
        per_device, mesh=mesh, in_specs=placed, out_specs=P("pix", "chan"), check_vma=False
    )
```

```python
import functools

import jax
import jax.numpy as jnp
from jax import lax
from jax.experimental import pallas as pl
from jax.experimental.pallas import tpu as pltpu
from jax.sharding import PartitionSpec as P

TERMS = 16
PASSES = 8
LANES = 128
WMAX = 1024
HALO = WMAX // 2
SEGMENTS = 8
CHUNK = 2048
WRITES = 4
HIGHEST = lax.Precision.HIGHEST


def exchange_order(n_chan):
    lead = n_chan * 75 // 128
    rest = [(17 * step) % n_chan for step in range(n_chan)]
    return [lead] + [device for device in rest if device != lead]


def chip_order(chips):
    lead = chips * 37 // 64
    rest = [(17 * step) % chips for step in range(chips)]
    return [lead] + [chip for chip in rest if chip != lead]


def device_order(chips):
    return [2 * chip + core for chip in chip_order(chips) for core in (1, 0)]


def legendre_rows(xvals):
    rows = [jnp.ones_like(xvals), xvals]
    for order in range(1, TERMS - 1):
        rows.append(
            ((2.0 * order + 1.0) * xvals * rows[order] - order * rows[order - 1])
            * (1.0 / (order + 1.0))
        )
    return rows


def inverse(matrix):
    row = lax.broadcasted_iota(jnp.int32, (TERMS, TERMS), 0)
    lane = lax.broadcasted_iota(jnp.int32, (TERMS, TERMS), 1)
    left, right = matrix, (row == lane).astype(jnp.float32)
    for k in range(TERMS):
        column = jnp.sum(jnp.where(lane == k, left, 0.0), axis=1, keepdims=True)
        scale = 1.0 / column[k : k + 1, :]
        left_k, right_k = left[k : k + 1, :] * scale, right[k : k + 1, :] * scale
        left = jnp.where(row == k, left_k, left - column * left_k)
        right = jnp.where(row == k, right_k, right - column * right_k)
    return right


def split(values):
    high = values.astype(jnp.bfloat16)
    return high, (values - high.astype(jnp.float32)).astype(jnp.bfloat16)


def dot(left, right):
    return jnp.dot(left, right, preferred_element_type=jnp.float32)


def prepare_kernel(start_ref, windows_ref, mask_ref, high_ref, low_ref, local_ref, widths_ref,
                   table, weighted):
    total = mask_ref.shape[1]
    row = lax.broadcasted_iota(jnp.int32, widths_ref.shape, 0)
    widths = jnp.zeros(widths_ref.shape, jnp.int32)
    for k in range(PASSES):
        widths = jnp.where(row == k, windows_ref[k], widths)
    widths_ref[...] = widths

    pix = local_ref.shape[0] // (2 * TERMS)
    index = lax.broadcasted_iota(jnp.int32, (pix, LANES), 1) + start_ref[0]
    xvals = (2.0 * index.astype(jnp.float32) + 1.0) / total - 1.0
    for term, values in enumerate(legendre_rows(xvals)):
        high, low = split(values)
        for half in range(2):
            rows = slice((half * TERMS + term) * pix, (half * TERMS + term + 1) * pix)
            local_ref[rows, :LANES], local_ref[rows, LANES:] = high, low

    gram = jnp.zeros((TERMS, TERMS), jnp.float32)
    for start in range(0, total, CHUNK):
        part = slice(start, start + CHUNK)
        index = lax.broadcasted_iota(jnp.int32, (1, CHUNK), 1) + start
        xvals = (2.0 * index.astype(jnp.float32) + 1.0) / total - 1.0
        keep = mask_ref[:, part].astype(jnp.float32)
        for term, values in enumerate(legendre_rows(xvals)):
            table[term : term + 1, part] = values
            weighted[term : term + 1, part] = values * keep
        gram = gram + lax.dot_general(
            weighted[:, part],
            table[:, part],
            (((1,), (1,)), ((), ())),
            precision=HIGHEST,
            preferred_element_type=jnp.float32,
        )
    inv = inverse(gram)
    count = total // SEGMENTS
    for segment in range(SEGMENTS):
        folded = jnp.dot(
            inv,
            weighted[:, segment * count : (segment + 1) * count],
            precision=HIGHEST,
            preferred_element_type=jnp.float32,
        )
        rows = slice(segment * TERMS, (segment + 1) * TERMS)
        high_ref[rows], low_ref[rows] = split(folded)


def snip_fit_kernel(widths_ref, spectra_ref, high_ref, low_ref, coef_ref,
                    first, second, hi, lo, widths, arrived):
    fetch = pltpu.make_async_copy(widths_ref, widths, arrived)
    fetch.start()
    n_chan, pix, _ = spectra_ref.shape
    blocks = n_chan // SEGMENTS
    rows = blocks * LANES
    half = blocks // 2
    order = device_order(n_chan // 2)
    place = [order.index(device) for device in range(n_chan)]
    lane = lax.broadcasted_iota(jnp.int32, (LANES, LANES), 1)

    def from_below(values):
        return jnp.where(
            lane[: values.shape[0]] < pix, jnp.inf, pltpu.roll(values, pix, 1)
        )

    def from_above(values):
        return jnp.where(
            lane[: values.shape[0]] >= LANES - pix, jnp.inf, pltpu.roll(values, LANES - pix, 1)
        )

    def turned(block):
        return jnp.concatenate(
            [spectra_ref[place[segment * blocks + block]] for segment in range(SEGMENTS)], axis=0
        ).T

    for block in range(half):
        low, high = turned(block), turned(block + half)
        first[pl.ds(HALO + block * LANES, LANES)] = jnp.minimum(
            low, 0.5 * (from_below(high) + high)
        )
        first[pl.ds(HALO + (block + half) * LANES, LANES)] = jnp.minimum(
            high, 0.5 * (low + from_above(low))
        )

    fetch.wait()
    source, target = first, second
    for k in range(1, PASSES):
        reach = max(8, WMAX >> k)
        for start in range(0, reach, LANES):
            count = min(LANES, reach)
            source[HALO - reach + start : HALO - reach + start + count] = from_below(
                source[HALO + rows - reach + start : HALO + rows - reach + start + count]
            )
            source[HALO + rows + start : HALO + rows + start + count] = from_above(
                source[HALO + start : HALO + start + count]
            )
        width = widths[k, 0] if k < PASSES - 1 else 1
        for start in range(0, rows, CHUNK):
            lower = source[pl.ds(HALO + start - width, CHUNK)]
            upper = source[pl.ds(HALO + start + width, CHUNK)]
            here = source[HALO + start : HALO + start + CHUNK]
            values = jnp.minimum(here, 0.5 * (lower + upper))
            if k < PASSES - 1:
                target[HALO + start : HALO + start + CHUNK] = values
            else:
                hi[start : start + CHUNK], lo[start : start + CHUNK] = split(values)
        source, target = target, source

    products = dot(high_ref[...], hi[...]) + (
        dot(low_ref[...], hi[...]) + dot(high_ref[...], lo[...])
    )
    lane = lax.broadcasted_iota(jnp.int32, (TERMS, LANES), 1)
    term = lax.broadcasted_iota(jnp.int32, (TERMS, LANES), 0)
    coefs = jnp.zeros((TERMS, LANES), jnp.float32)
    for segment in range(SEGMENTS):
        coefs = coefs + jnp.where(
            (lane // pix) == segment, products[segment * TERMS : (segment + 1) * TERMS], 0.0
        )
    shift = LANES // 2
    while shift >= pix:
        coefs = coefs + pltpu.roll(coefs, shift, 1)
        shift //= 2
    coefs = jnp.where((lane // pix) == (term % 8), coefs, 0.0)
    coef_ref[0:1] = jnp.sum(coefs[:8], axis=0, keepdims=True)
    coef_ref[1:2] = jnp.sum(coefs[8:], axis=0, keepdims=True)


def subtract_kernel(owner, coef_ref, local_ref, cube_ref, out_ref, left, result, sent):
    core = lax.rem(lax.axis_index("chan"), 2)
    which = 1 - core if owner == "own" else core
    chips, _, pix, _ = cube_ref.shape
    row = lax.broadcasted_iota(jnp.int32, (pix, LANES), 0)
    lane = lax.broadcasted_iota(jnp.int32, (pix, LANES), 1)
    own = (lane & (pix - 1)) == row
    step = chips // WRITES
    copies = []
    for block in range(WRITES):
        slot = left.at[block % 2]
        for u in range(step):
            for half in range(2):
                values = coef_ref[block * step + u, half : half + 1, :]
                high, low = split(jnp.where(own, jnp.broadcast_to(values, own.shape), 0.0))
                rows = slice(u * pix, (u + 1) * pix)
                slot[rows, half * LANES : (half + 1) * LANES] = high
                slot[rows, (2 + half) * LANES : (3 + half) * LANES] = low
        fitted = dot(slot[...], local_ref[...])
        fitted = (fitted[:, :LANES] + fitted[:, LANES:]).reshape(step, pix, LANES)
        part = pl.ds(block * step, step)
        result[part] = cube_ref[part, which] - fitted
        copy = pltpu.make_async_copy(result.at[part], out_ref.at[part, which], sent.at[block])
        copy.start()
        copies.append(copy)
    for copy in copies:
        copy.wait()


def subtract_rest_kernel(coef_ref, local_ref, cube_ref, begun_ref, out_ref, left, result, sent):
    subtract_kernel("other", coef_ref, local_ref, cube_ref, out_ref, left, result, sent)


def params():
    return pltpu.CompilerParams(vmem_limit_bytes=32 * 1024 * 1024)


def per_device(cube, windows, mask):
    ch_dev = cube.shape[1]
    n_chan = lax.axis_size("chan")
    total = ch_dev * n_chan
    pix = cube.shape[0] // n_chan
    vmem = pl.BlockSpec(memory_space=pltpu.VMEM)
    smem = pl.BlockSpec(memory_space=pltpu.SMEM)

    chips = n_chan // 2
    spectra = lax.all_to_all(
        cube.reshape(n_chan, pix, ch_dev),
        "chan",
        split_axis=0,
        concat_axis=0,
        tiled=True,
        axis_index_groups=[device_order(chips)],
    )
    rows = total // SEGMENTS
    start = (lax.axis_index("chan") * ch_dev).astype(jnp.int32).reshape(1)
    high, low, local, widths = pl.pallas_call(
        prepare_kernel,
        out_shape=[jax.ShapeDtypeStruct((SEGMENTS * TERMS, rows), jnp.bfloat16)] * 2
        + [
            jax.ShapeDtypeStruct((2 * TERMS * pix, 2 * LANES), jnp.bfloat16),
            jax.ShapeDtypeStruct((PASSES, LANES), jnp.int32),
        ],
        in_specs=[smem, smem, vmem],
        out_specs=[vmem] * 4,
        scratch_shapes=[pltpu.VMEM((TERMS, total), jnp.float32)] * 2,
        compiler_params=params(),
        cost_estimate=pl.CostEstimate(
            flops=20_000_000, bytes_accessed=total * 68, transcendentals=0
        ),
    )(start, windows, mask.reshape(1, total))
    coefs = pl.pallas_call(
        snip_fit_kernel,
        out_shape=jax.ShapeDtypeStruct((2, LANES), jnp.float32),
        in_specs=[pl.BlockSpec(memory_space=pl.ANY), vmem, vmem, vmem],
        out_specs=vmem,
        scratch_shapes=[pltpu.VMEM((rows + 2 * HALO, LANES), jnp.float32)] * 2
        + [pltpu.VMEM((rows, LANES), jnp.bfloat16)] * 2
        + [pltpu.SMEM((PASSES, LANES), jnp.int32), pltpu.SemaphoreType.DMA],
        compiler_params=params(),
    )(widths, spectra, high, low)

    mine = lax.all_to_all(
        jnp.broadcast_to(coefs[None], (chips,) + coefs.shape),
        "chan",
        split_axis=0,
        concat_axis=0,
        tiled=True,
        axis_index_groups=[[2 * chip + core for chip in chip_order(chips)] for core in range(2)],
    )
    other = lax.ppermute(mine, "chan", [(i, i ^ 1) for i in range(n_chan)])
    cube = cube.reshape(chips, 2, pix, ch_dev)
    anywhere = pl.BlockSpec(memory_space=pl.ANY)
    common = dict(
        out_shape=jax.ShapeDtypeStruct(cube.shape, jnp.float32),
        out_specs=anywhere,
        scratch_shapes=[
            pltpu.VMEM((2, chips // WRITES * pix, 4 * LANES), jnp.bfloat16),
            pltpu.VMEM((chips, pix, ch_dev), jnp.float32),
            pltpu.SemaphoreType.DMA((WRITES,)),
        ],
        compiler_params=params(),
        cost_estimate=pl.CostEstimate(
            flops=1_000_000_000, bytes_accessed=cube.size * 4, transcendentals=0
        ),
    )
    begun = pl.pallas_call(
        functools.partial(subtract_kernel, "own"), in_specs=[vmem] * 3, **common
    )(mine, local, cube)
    whole = pl.pallas_call(
        subtract_rest_kernel,
        in_specs=[vmem] * 3 + [anywhere],
        input_output_aliases={3: 0},
        **common,
    )(other, local, cube, begun)
    return whole.reshape(n_chan * pix, ch_dev)


def solution(mesh):
    placed = (P("pix", "chan"), P(), P())
    return jax.shard_map(
        per_device, mesh=mesh, in_specs=placed, out_specs=P("pix", "chan"), check_vma=False
    )
```

```python
import functools

import jax
import jax.numpy as jnp
from jax import lax
from jax.experimental import pallas as pl
from jax.experimental.pallas import tpu as pltpu
from jax.sharding import PartitionSpec as P

TERMS = 16
PASSES = 8
LANES = 128
WMAX = 1024
HALO = WMAX // 2
SEGMENTS = 8
CHUNK = 2048
WRITES = 8
HIGHEST = lax.Precision.HIGHEST


def exchange_order(n_chan):
    lead = n_chan * 75 // 128
    rest = [(17 * step) % n_chan for step in range(n_chan)]
    return [lead] + [device for device in rest if device != lead]


def chip_order(chips):
    lead = chips * 37 // 64
    rest = [(17 * step) % chips for step in range(chips)]
    return [lead] + [chip for chip in rest if chip != lead]


def device_order(chips):
    return [2 * chip + core for chip in chip_order(chips) for core in (1, 0)]


def legendre_rows(xvals):
    rows = [jnp.ones_like(xvals), xvals]
    for order in range(1, TERMS - 1):
        rows.append(
            ((2.0 * order + 1.0) * xvals * rows[order] - order * rows[order - 1])
            * (1.0 / (order + 1.0))
        )
    return rows


def inverse(matrix):
    row = lax.broadcasted_iota(jnp.int32, (TERMS, TERMS), 0)
    lane = lax.broadcasted_iota(jnp.int32, (TERMS, TERMS), 1)
    left, right = matrix, (row == lane).astype(jnp.float32)
    for k in range(TERMS):
        column = jnp.sum(jnp.where(lane == k, left, 0.0), axis=1, keepdims=True)
        scale = 1.0 / column[k : k + 1, :]
        left_k, right_k = left[k : k + 1, :] * scale, right[k : k + 1, :] * scale
        left = jnp.where(row == k, left_k, left - column * left_k)
        right = jnp.where(row == k, right_k, right - column * right_k)
    return right


def split(values):
    high = values.astype(jnp.bfloat16)
    return high, (values - high.astype(jnp.float32)).astype(jnp.bfloat16)


def dot(left, right):
    return jnp.dot(left, right, preferred_element_type=jnp.float32)


def prepare_kernel(start_ref, windows_ref, mask_ref, high_ref, low_ref, local_ref, widths_ref,
                   table, weighted):
    total = mask_ref.shape[1]
    row = lax.broadcasted_iota(jnp.int32, widths_ref.shape, 0)
    widths = jnp.zeros(widths_ref.shape, jnp.int32)
    for k in range(PASSES):
        widths = jnp.where(row == k, windows_ref[k], widths)
    widths_ref[...] = widths

    pix = local_ref.shape[0] // (2 * TERMS)
    index = lax.broadcasted_iota(jnp.int32, (pix, LANES), 1) + start_ref[0]
    xvals = (2.0 * index.astype(jnp.float32) + 1.0) / total - 1.0
    for term, values in enumerate(legendre_rows(xvals)):
        high, low = split(values)
        for half in range(2):
            rows = slice((half * TERMS + term) * pix, (half * TERMS + term + 1) * pix)
            local_ref[rows, :LANES], local_ref[rows, LANES:] = high, low

    gram = jnp.zeros((TERMS, TERMS), jnp.float32)
    for start in range(0, total, CHUNK):
        part = slice(start, start + CHUNK)
        index = lax.broadcasted_iota(jnp.int32, (1, CHUNK), 1) + start
        xvals = (2.0 * index.astype(jnp.float32) + 1.0) / total - 1.0
        keep = mask_ref[:, part].astype(jnp.float32)
        for term, values in enumerate(legendre_rows(xvals)):
            table[term : term + 1, part] = values
            weighted[term : term + 1, part] = values * keep
        gram = gram + lax.dot_general(
            weighted[:, part],
            table[:, part],
            (((1,), (1,)), ((), ())),
            precision=HIGHEST,
            preferred_element_type=jnp.float32,
        )
    inv = inverse(gram)
    count = total // SEGMENTS
    for segment in range(SEGMENTS):
        folded = jnp.dot(
            inv,
            weighted[:, segment * count : (segment + 1) * count],
            precision=HIGHEST,
            preferred_element_type=jnp.float32,
        )
        rows = slice(segment * TERMS, (segment + 1) * TERMS)
        high_ref[rows], low_ref[rows] = split(folded)


def snip_fit_kernel(widths_ref, spectra_ref, high_ref, low_ref, coef_ref,
                    first, second, hi, lo, widths, arrived):
    fetch = pltpu.make_async_copy(widths_ref, widths, arrived)
    fetch.start()
    n_chan, pix, _ = spectra_ref.shape
    blocks = n_chan // SEGMENTS
    rows = blocks * LANES
    half = blocks // 2
    order = device_order(n_chan // 2)
    place = [order.index(device) for device in range(n_chan)]
    lane = lax.broadcasted_iota(jnp.int32, (LANES, LANES), 1)

    def from_below(values):
        return jnp.where(
            lane[: values.shape[0]] < pix, jnp.inf, pltpu.roll(values, pix, 1)
        )

    def from_above(values):
        return jnp.where(
            lane[: values.shape[0]] >= LANES - pix, jnp.inf, pltpu.roll(values, LANES - pix, 1)
        )

    def turned(block):
        return jnp.concatenate(
            [spectra_ref[place[segment * blocks + block]] for segment in range(SEGMENTS)], axis=0
        ).T

    for block in range(half):
        low, high = turned(block), turned(block + half)
        first[pl.ds(HALO + block * LANES, LANES)] = jnp.minimum(
            low, 0.5 * (from_below(high) + high)
        )
        first[pl.ds(HALO + (block + half) * LANES, LANES)] = jnp.minimum(
            high, 0.5 * (low + from_above(low))
        )

    fetch.wait()
    source, target = first, second
    for k in range(1, PASSES):
        reach = max(8, WMAX >> k)
        for start in range(0, reach, LANES):
            count = min(LANES, reach)
            source[HALO - reach + start : HALO - reach + start + count] = from_below(
                source[HALO + rows - reach + start : HALO + rows - reach + start + count]
            )
            source[HALO + rows + start : HALO + rows + start + count] = from_above(
                source[HALO + start : HALO + start + count]
            )
        width = widths[k, 0] if k < PASSES - 1 else 1
        for start in range(0, rows, CHUNK):
            lower = source[pl.ds(HALO + start - width, CHUNK)]
            upper = source[pl.ds(HALO + start + width, CHUNK)]
            here = source[HALO + start : HALO + start + CHUNK]
            values = jnp.minimum(here, 0.5 * (lower + upper))
            if k < PASSES - 1:
                target[HALO + start : HALO + start + CHUNK] = values
            else:
                hi[start : start + CHUNK], lo[start : start + CHUNK] = split(values)
        source, target = target, source

    products = dot(high_ref[...], hi[...]) + (
        dot(low_ref[...], hi[...]) + dot(high_ref[...], lo[...])
    )
    lane = lax.broadcasted_iota(jnp.int32, (TERMS, LANES), 1)
    term = lax.broadcasted_iota(jnp.int32, (TERMS, LANES), 0)
    coefs = jnp.zeros((TERMS, LANES), jnp.float32)
    for segment in range(SEGMENTS):
        coefs = coefs + jnp.where(
            (lane // pix) == segment, products[segment * TERMS : (segment + 1) * TERMS], 0.0
        )
    shift = LANES // 2
    while shift >= pix:
        coefs = coefs + pltpu.roll(coefs, shift, 1)
        shift //= 2
    coefs = jnp.where((lane // pix) == (term % 8), coefs, 0.0)
    coef_ref[0:1] = jnp.sum(coefs[:8], axis=0, keepdims=True)
    coef_ref[1:2] = jnp.sum(coefs[8:], axis=0, keepdims=True)


def subtract_kernel(owner, coef_ref, local_ref, cube_ref, out_ref, left, result, sent,
                    high_coef, low_coef):
    core = lax.rem(lax.axis_index("chan"), 2)
    which = 1 - core if owner == "own" else core
    chips, _, pix, _ = cube_ref.shape
    row = lax.broadcasted_iota(jnp.int32, (pix, LANES), 0)
    lane = lax.broadcasted_iota(jnp.int32, (pix, LANES), 1)
    own = (lane & (pix - 1)) == row
    step = chips // WRITES
    upper, lower = split(coef_ref[...])
    high_coef[...], low_coef[...] = upper.astype(jnp.float32), lower.astype(jnp.float32)
    copies = []
    for block in range(WRITES):
        slot = left.at[block % 2]
        for u in range(step):
            for half in range(2):
                rows = slice(u * pix, (u + 1) * pix)
                for at, part in ((half, high_coef), (2 + half, low_coef)):
                    values = jnp.broadcast_to(
                        part[block * step + u, half : half + 1, :], own.shape
                    )
                    slot[rows, at * LANES : (at + 1) * LANES] = jnp.where(
                        own, values, 0.0
                    ).astype(jnp.bfloat16)
        fitted = dot(slot[...], local_ref[...])
        fitted = (fitted[:, :LANES] + fitted[:, LANES:]).reshape(step, pix, LANES)
        part = pl.ds(block * step, step)
        result[part] = cube_ref[part, which] - fitted
        copy = pltpu.make_async_copy(result.at[part], out_ref.at[part, which], sent.at[block])
        copy.start()
        copies.append(copy)
    for copy in copies:
        copy.wait()


def subtract_rest_kernel(coef_ref, local_ref, cube_ref, begun_ref, out_ref, *scratch):
    subtract_kernel("other", coef_ref, local_ref, cube_ref, out_ref, *scratch)


def params():
    return pltpu.CompilerParams(vmem_limit_bytes=32 * 1024 * 1024)


def per_device(cube, windows, mask):
    ch_dev = cube.shape[1]
    n_chan = lax.axis_size("chan")
    total = ch_dev * n_chan
    pix = cube.shape[0] // n_chan
    vmem = pl.BlockSpec(memory_space=pltpu.VMEM)
    smem = pl.BlockSpec(memory_space=pltpu.SMEM)

    chips = n_chan // 2
    spectra = lax.all_to_all(
        cube.reshape(n_chan, pix, ch_dev),
        "chan",
        split_axis=0,
        concat_axis=0,
        tiled=True,
        axis_index_groups=[device_order(chips)],
    )
    rows = total // SEGMENTS
    start = (lax.axis_index("chan") * ch_dev).astype(jnp.int32).reshape(1)
    high, low, local, widths = pl.pallas_call(
        prepare_kernel,
        out_shape=[jax.ShapeDtypeStruct((SEGMENTS * TERMS, rows), jnp.bfloat16)] * 2
        + [
            jax.ShapeDtypeStruct((2 * TERMS * pix, 2 * LANES), jnp.bfloat16),
            jax.ShapeDtypeStruct((PASSES, LANES), jnp.int32),
        ],
        in_specs=[smem, smem, vmem],
        out_specs=[vmem] * 4,
        scratch_shapes=[pltpu.VMEM((TERMS, total), jnp.float32)] * 2,
        compiler_params=params(),
        cost_estimate=pl.CostEstimate(
            flops=20_000_000, bytes_accessed=total * 68, transcendentals=0
        ),
    )(start, windows, mask.reshape(1, total))
    coefs = pl.pallas_call(
        snip_fit_kernel,
        out_shape=jax.ShapeDtypeStruct((2, LANES), jnp.float32),
        in_specs=[pl.BlockSpec(memory_space=pl.ANY), vmem, vmem, vmem],
        out_specs=vmem,
        scratch_shapes=[pltpu.VMEM((rows + 2 * HALO, LANES), jnp.float32)] * 2
        + [pltpu.VMEM((rows, LANES), jnp.bfloat16)] * 2
        + [pltpu.SMEM((PASSES, LANES), jnp.int32), pltpu.SemaphoreType.DMA],
        compiler_params=params(),
    )(widths, spectra, high, low)

    mine = lax.all_to_all(
        jnp.broadcast_to(coefs[None], (chips,) + coefs.shape),
        "chan",
        split_axis=0,
        concat_axis=0,
        tiled=True,
        axis_index_groups=[[2 * chip + core for chip in chip_order(chips)] for core in range(2)],
    )
    other = lax.ppermute(mine, "chan", [(i, i ^ 1) for i in range(n_chan)])
    cube = cube.reshape(chips, 2, pix, ch_dev)
    anywhere = pl.BlockSpec(memory_space=pl.ANY)
    common = dict(
        out_shape=jax.ShapeDtypeStruct(cube.shape, jnp.float32),
        out_specs=anywhere,
        scratch_shapes=[
            pltpu.VMEM((2, chips // WRITES * pix, 4 * LANES), jnp.bfloat16),
            pltpu.VMEM((chips, pix, ch_dev), jnp.float32),
            pltpu.SemaphoreType.DMA((WRITES,)),
        ]
        + [pltpu.VMEM(mine.shape, jnp.float32)] * 2,
        compiler_params=params(),
        cost_estimate=pl.CostEstimate(
            flops=1_000_000_000, bytes_accessed=cube.size * 4, transcendentals=0
        ),
    )
    begun = pl.pallas_call(
        functools.partial(subtract_kernel, "own"), in_specs=[vmem] * 3, **common
    )(mine, local, cube)
    whole = pl.pallas_call(
        subtract_rest_kernel,
        in_specs=[vmem] * 3 + [anywhere],
        input_output_aliases={3: 0},
        **common,
    )(other, local, cube, begun)
    return whole.reshape(n_chan * pix, ch_dev)


def solution(mesh):
    placed = (P("pix", "chan"), P(), P())
    return jax.shard_map(
        per_device, mesh=mesh, in_specs=placed, out_specs=P("pix", "chan"), check_vma=False
    )
```
